32 devices in a mesh: seq: 4 (over x, core), dp: 8 (over z, y).
Axes of the slice: x: 2, y: 2, z: 4, core: 2. Of those that a mesh axis runs over, the one named last changes fastest.
Arguments:
- queries: bfloat16 [8, 512, 4096], P('dp', 'seq'), may hold values from -4.5 to 4.5
- rotated_key_matrix: bfloat16 [8, 512, 1024], P('dp', 'seq'), may hold values from -4.5 to 4.5
- value_matrix: bfloat16 [8, 512, 1024], P('dp', 'seq'), may hold values from -6 to 6
- out_weight: bfloat16 [4096, 2048], P('seq'), may hold values from -0.09375 to 0.09375
- out_grad: bfloat16 [8, 512, 2048], P('dp', 'seq'), may hold values from -6 to 6
- lengths: int32 [8, 16], P('dp'), may hold values from 1 to 128, 512 in all within a row
- pack_order: int32 [8, 16], P('dp'), may hold values from 0 to 15, each once within a row
Outputs:
- layer_out: bfloat16 [8, 512, 2048], P('dp', 'seq')
- query_grad: bfloat16 [8, 512, 4096], P('dp', 'seq')
- key_grad: bfloat16 [8, 512, 1024], P('dp', 'seq')
- value_grad: bfloat16 [8, 512, 1024], P('dp', 'seq')
- weight_grad: float32 [4096, 2048], P('seq', 'dp')
The draws below stay inside these ranges and needn't reach their ends.
Inputs may be any that keep to these rules, and one draw needn't show every extreme that they name: The 16 lengths of a window sum to 512; the longest is 128. `pack_order`: each row names every sample once.
All inputs are finite; a program needn't handle non-finite values.
Results may differ from the reference program's by a relative error of at most 0.017.
Values may be sent and summed in bfloat16 or wider, within the bound.
A program may use at most 128 MiB of HBM per device.

```python
import math
import jax
import jax.numpy as jnp
import numpy as np
from jax import lax

D = 2048
QUERY_HEADS = 32
KEY_VALUE_HEADS = 8
HEAD_SIZE = 128
NSAMP = 16
WINDOW_TOKENS = 512
WINDOW_COUNT = 8
MOST = 128
N_SEQ = 4


def draw_queries(key, part):
    return jax.random.truncated_normal(jax.random.fold_in(key, 105), -4.5, 4.5, (WINDOW_COUNT, WINDOW_TOKENS, QUERY_HEADS * HEAD_SIZE), jnp.float32).astype(jnp.bfloat16)


def draw_rotated_key_matrix(key, part):
    return jax.random.truncated_normal(jax.random.fold_in(key, 107), -4.5, 4.5, (WINDOW_COUNT, WINDOW_TOKENS, KEY_VALUE_HEADS * HEAD_SIZE), jnp.float32).astype(jnp.bfloat16)


def with_spikes(drawn, own_key, source, target, blocks, factor):
    owner, partner = [(jnp.arange(drawn.shape[axis_at]) // (drawn.shape[axis_at] // blocks)).reshape([-1 if axis == axis_at else 1 for axis in range(drawn.ndim)]) for axis_at in (source, target)]
    chosen = jax.random.permutation(own_key, blocks)[partner]
    strong = (owner == chosen) | (owner == (partner + blocks // 2) % blocks)
    return jnp.where(strong, factor * drawn, drawn)


def block_scale(stream_key, shape, split, least, top_value):
    factor_of, own = 1.0, jax.random.fold_in(stream_key, 6)
    for dim, blocks in split:
        draws = jnp.exp(jax.random.uniform(jax.random.fold_in(own, dim), (blocks,), jnp.float32, least / len(split), top_value / len(split)))
        factor_of = factor_of * jnp.repeat(draws, shape[dim] // blocks).reshape([-1 if axis == dim else 1 for axis in range(len(shape))])
    return factor_of


def profile(number_of, total, limit, slope):
    loads = [(1 << 20) // math.isqrt(rank ** slope) + 1 for rank in range(2, number_of + 1)]
    spare, counts = total - limit - (number_of - 1), [1] * (number_of - 1)
    while spare > 0:
        candidates = [i for i in range(number_of - 1) if counts[i] < limit]
        mass, budget = sum([loads[i] for i in candidates]), spare
        for i in candidates:
            more = min(limit - counts[i], max(1, budget * loads[i] // mass), spare)
            counts[i] = counts[i] + more
            spare = spare - more
    return np.array([limit] + counts)


def uneven(key, number_of, total, bound, slope):
    if number_of == 2:
        one = jax.random.randint(key, (), max(1, total - bound), min(bound, total - 1) + 1)
        return jnp.stack([one, total - one])
    tallies = jnp.asarray(profile(number_of, total, bound, slope), jnp.int32)
    pairs = (number_of - 1) // 2
    donor, sink = tallies[1:1 + 2 * pairs:2], tallies[2:2 + 2 * pairs:2]
    margin = jnp.minimum(donor - 1, bound - sink)
    shifted = jax.random.randint(jax.random.fold_in(key, 1), (pairs,), 0, 1 << 20) % (margin + 1)
    tallies = tallies.at[1:1 + 2 * pairs:2].set(donor - shifted).at[2:2 + 2 * pairs:2].set(sink + shifted)
    return tallies[jax.random.permutation(jax.random.fold_in(key, 2), number_of)]


def centred(rng, extent, deviation, most, split=(), kind=jnp.bfloat16):
    loudness = block_scale(rng, extent, split, -0.22, 0.18) if split else 1.0
    result = jax.random.normal(rng, extent, jnp.float32) * deviation * loudness
    return jnp.minimum(jnp.maximum(result, -most), most).astype(kind)


def heavy_noise(key, extent, deviation, bound, shards, heavy, kind=jnp.bfloat16):
    entries = deviation * jax.random.normal(key, extent, jnp.float32)
    if shards:
        entries = entries * block_scale(key, extent, shards, -0.22, 0.18)
    return jnp.clip(with_spikes(entries, jax.random.fold_in(key, 3), *heavy), -bound, bound).astype(kind)


def setup_inputs(seed: int = 0) -> dict:
    keys = jax.random.split(jax.random.key(seed), 8)
    queries = draw_queries(jax.random.fold_in(keys[7], 71), 0)
    rotated_key_matrix = draw_rotated_key_matrix(jax.random.fold_in(keys[7], 71), 0)
    value_matrix = centred(keys[2], (WINDOW_COUNT, WINDOW_TOKENS, KEY_VALUE_HEADS * HEAD_SIZE), 1.0, 6.0, ((0, 8), (1, 4)))
    out_weight = centred(keys[3], (QUERY_HEADS * HEAD_SIZE, D), (QUERY_HEADS * HEAD_SIZE) ** -0.5, 0.09375, ((0, 4),))
    out_grad = heavy_noise(keys[4], (WINDOW_COUNT, WINDOW_TOKENS, D), 1.0, 6.0, ((0, 8), (1, 4)), (0, 2, 8, 2.0))
    lengths = jax.vmap(lambda own: uneven(own, NSAMP, WINDOW_TOKENS, MOST, 2))(jax.random.split(keys[5], WINDOW_COUNT)).reshape((WINDOW_COUNT, NSAMP)).astype(jnp.int32)
    pack_order = jax.vmap(lambda own: jax.random.permutation(own, NSAMP))(jax.random.split(keys[6], WINDOW_COUNT)).reshape((WINDOW_COUNT, NSAMP)).astype(jnp.int32)
    return {"queries": queries, "rotated_key_matrix": rotated_key_matrix, "value_matrix": value_matrix, "out_weight": out_weight, "out_grad": out_grad, "lengths": lengths, "pack_order": pack_order}


def row_starts(lengths, pack_order, win_rows):
    samples = lengths.shape[0]
    picked = jnp.sum(jnp.where(pack_order[:, None] == jnp.arange(samples, dtype=jnp.int32)[None, :], lengths[None, :], 0), axis=1, dtype=jnp.int32)
    seg_ends = jnp.cumsum(picked, dtype=jnp.int32)
    places = jnp.arange(win_rows, dtype=jnp.int32)
    return jnp.sum(jnp.where(seg_ends[None, :] <= places[:, None], picked[None, :], 0), axis=1, dtype=jnp.int32)


def reference(queries, rotated_key_matrix, value_matrix, out_weight, out_grad, lengths, pack_order):
    group_width = QUERY_HEADS // KEY_VALUE_HEADS
    head_scale = HEAD_SIZE ** -0.5
    group_cols = QUERY_HEADS * HEAD_SIZE // N_SEQ
    wo_float = out_weight.astype(jnp.float32)
    wo_groups = wo_float.reshape(N_SEQ, group_cols, D)

    def window(wo_grad, window_in):
        query_window, key_window, value_window, g_win, len_win, ord_win = window_in
        starts = row_starts(len_win, ord_win, WINDOW_TOKENS)
        places = jnp.arange(WINDOW_TOKENS, dtype=jnp.int32)
        visible = (places[None, :] >= starts[:, None]) & (places[None, :] <= places[:, None])
        query_head_rows = query_window.reshape(WINDOW_TOKENS, KEY_VALUE_HEADS, group_width, HEAD_SIZE).astype(jnp.float32)
        key_head_rows = key_window.reshape(WINDOW_TOKENS, KEY_VALUE_HEADS, HEAD_SIZE).astype(jnp.float32)
        value_head_rows = value_window.reshape(WINDOW_TOKENS, KEY_VALUE_HEADS, HEAD_SIZE).astype(jnp.float32)
        scores = jnp.einsum('qkgd,skd->kgqs', query_head_rows, key_head_rows) * head_scale
        row_max = jnp.max(jnp.where(visible, scores, -jnp.inf), axis=-1, keepdims=True)
        expd = jnp.where(visible, jnp.exp(scores - row_max), 0.0)
        row_sum = jnp.sum(expd, axis=-1, keepdims=True)
        attn_prob = expd / row_sum
        half_probability = attn_prob.astype(jnp.bfloat16)
        attn_out = jnp.einsum('kgqs,skd->qkgd', half_probability.astype(jnp.float32), value_head_rows).astype(jnp.bfloat16)
        a_flat = attn_out.reshape(WINDOW_TOKENS, QUERY_HEADS * HEAD_SIZE)
        pieces = jnp.einsum('tnc,ncd->tnd', a_flat.reshape(WINDOW_TOKENS, N_SEQ, group_cols).astype(jnp.float32), wo_groups)
        pieces = lax.optimization_barrier(pieces.astype(jnp.bfloat16)).astype(jnp.float32)
        y_out = jnp.sum(pieces, axis=1).astype(jnp.bfloat16)
        wo_grad = wo_grad + jnp.dot(a_flat.T, g_win, preferred_element_type=jnp.float32)
        attention_grad = jnp.dot(g_win, out_weight.T, preferred_element_type=jnp.float32).astype(jnp.bfloat16)
        attention_grad = attention_grad.reshape(WINDOW_TOKENS, KEY_VALUE_HEADS, group_width, HEAD_SIZE).astype(jnp.float32)
        row_dot = jnp.sum(attention_grad * attn_out.astype(jnp.float32), axis=-1)
        row_dot = jnp.transpose(row_dot, (1, 2, 0))[..., None]
        d_prob = jnp.einsum('qkgd,skd->kgqs', attention_grad, value_head_rows)
        score_gradient = (attn_prob * (d_prob - row_dot) * head_scale).astype(jnp.bfloat16).astype(jnp.float32)
        d_q = jnp.einsum('kgqs,skd->qkgd', score_gradient, key_head_rows).astype(jnp.bfloat16).reshape(WINDOW_TOKENS, QUERY_HEADS * HEAD_SIZE)
        key_gradient = jnp.einsum('ubnh,nubr->hur', score_gradient, query_head_rows).astype(jnp.bfloat16).reshape(WINDOW_TOKENS, KEY_VALUE_HEADS * HEAD_SIZE)
        value_gradient = jnp.einsum('ubnh,nubr->hur', half_probability.astype(jnp.float32), attention_grad).astype(jnp.bfloat16).reshape(WINDOW_TOKENS, KEY_VALUE_HEADS * HEAD_SIZE)
        return wo_grad, (y_out, d_q, key_gradient, value_gradient)

    wo_grad, (layer_out, query_grad, key_grad, value_grad) = lax.scan(
        window, jnp.zeros((QUERY_HEADS * HEAD_SIZE, D), jnp.float32),
        (queries, rotated_key_matrix, value_matrix, out_grad, lengths, pack_order))
    return layer_out, query_grad, key_grad, value_grad, wo_grad
```

```python
import functools

import jax
import jax.numpy as jnp
from jax import lax
from jax.experimental import pallas as pl
from jax.experimental.pallas import tpu as pltpu
from jax.sharding import PartitionSpec as P

QUERY_HEADS = 32
KEY_VALUE_HEADS = 8
HEAD_SIZE = 128
GROUP = QUERY_HEADS // KEY_VALUE_HEADS
SCALE = HEAD_SIZE**-0.5


def row_starts(lengths, pack_order, win_rows):
    samples = lengths.shape[0]
    picked = jnp.sum(
        jnp.where(
            pack_order[:, None] == jnp.arange(samples, dtype=jnp.int32)[None, :],
            lengths[None, :],
            0,
        ),
        axis=1,
        dtype=jnp.int32,
    )
    at = jnp.arange(samples, dtype=jnp.int32)
    seg_ends = jnp.sum(jnp.where(at[None, :] <= at[:, None], picked[None, :], 0), axis=1)
    places = jnp.arange(win_rows, dtype=jnp.int32)
    return jnp.sum(
        jnp.where(seg_ends[None, :] <= places[:, None], picked[None, :], 0), axis=1, dtype=jnp.int32
    )


def nt(a, b):
    return lax.dot_general(a, b, (((1,), (1,)), ((), ())), preferred_element_type=jnp.float32)


def tn(a, b):
    return lax.dot_general(a, b, (((0,), (0,)), ((), ())), preferred_element_type=jnp.float32)


def stack_heads(x):
    return jnp.concatenate(
        [x[:, j * HEAD_SIZE : (j + 1) * HEAD_SIZE] for j in range(GROUP)], axis=0
    )


def unstack_heads(x, rows):
    return jnp.concatenate([x[j * rows : (j + 1) * rows] for j in range(GROUP)], axis=1)


def forward_kernel(q_ref, k_ref, v_ref, first_ref, a_ref, p_ref):
    rows, wide = q_ref.shape[0], k_ref.shape[0]
    back = wide - rows
    col = lax.broadcasted_iota(jnp.int32, (rows, wide), 1)
    row = lax.broadcasted_iota(jnp.int32, (rows, wide), 0) + back
    visible = (col >= first_ref[...]) & (col <= row)
    hidden = jnp.where(visible, 0.0, -jnp.inf)
    hidden = jnp.concatenate([hidden] * GROUP, axis=0)
    scores = nt(stack_heads(q_ref[...]), k_ref[...]) * SCALE + hidden
    e = jnp.exp(scores - jnp.max(scores, axis=-1, keepdims=True))
    p = (e / jnp.sum(e, axis=-1, keepdims=True)).astype(jnp.bfloat16)
    p_ref[0] = p
    a = jnp.dot(p, v_ref[...], preferred_element_type=jnp.float32).astype(jnp.bfloat16)
    a_ref[...] = unstack_heads(a, rows)


def backward_kernel(q_ref, k_ref, v_ref, a_ref, g_ref, p_ref, dq_ref, dk_ref, dv_ref):
    rows = q_ref.shape[0]
    q, g = stack_heads(q_ref[...]), stack_heads(g_ref[...])
    a = stack_heads(a_ref[...])
    p = p_ref[0]
    dot = jnp.sum(a.astype(jnp.float32) * g.astype(jnp.float32), axis=-1, keepdims=True)
    dp = nt(g, v_ref[...])
    ds = (p.astype(jnp.float32) * (dp - dot) * SCALE).astype(jnp.bfloat16)
    dq = jnp.dot(ds, k_ref[...], preferred_element_type=jnp.float32).astype(jnp.bfloat16)
    dq_ref[...] = unstack_heads(dq, rows)
    dk_ref[...] = tn(ds, q).astype(dk_ref.dtype)
    dv_ref[...] = tn(p, g).astype(dv_ref.dtype)


def local(n_seq, n_dp, queries, keys, values, out_weight, out_grad, lengths, pack_order):
    q, k, v, g = queries[0], keys[0], values[0], out_grad[0]
    rows = q.shape[0]
    win = rows * n_seq
    longest = win // 4
    halo = -(-(longest - 1) // rows)
    me = lax.axis_index("seq")
    starts = row_starts(lengths[0], pack_order[0], win)
    first = lax.dynamic_slice_in_dim(starts, me * rows, rows, 0) - (me - halo) * rows
    first = first[:, None]

    kv = jnp.concatenate([k, v], axis=1)
    pieces = [kv]
    for j in range(1, halo + 1):
        pieces.insert(0, lax.ppermute(kv, "seq", [(i, i + j) for i in range(n_seq - j)]))
    kv_all = jnp.concatenate(pieces, axis=0)
    wide = kv_all.shape[0]
    g_all = lax.all_gather(g, "seq", axis=0, tiled=True)

    kvw = KEY_VALUE_HEADS * HEAD_SIZE
    gw = GROUP * HEAD_SIZE
    q_spec = pl.BlockSpec((rows, gw), lambda i: (0, i))
    k_spec = pl.BlockSpec((wide, HEAD_SIZE), lambda i: (0, i))
    v_spec = pl.BlockSpec((wide, HEAD_SIZE), lambda i: (0, i + KEY_VALUE_HEADS))
    p_spec = pl.BlockSpec((1, GROUP * rows, wide), lambda i: (i, 0, 0))
    params = pltpu.CompilerParams(vmem_limit_bytes=32 << 20)
    a, p = pl.pallas_call(
        forward_kernel,
        grid=(KEY_VALUE_HEADS,),
        in_specs=[q_spec, k_spec, v_spec, pl.BlockSpec((rows, 1), lambda i: (0, 0))],
        out_specs=[q_spec, p_spec],
        out_shape=[
            jax.ShapeDtypeStruct(q.shape, jnp.bfloat16),
            jax.ShapeDtypeStruct((KEY_VALUE_HEADS, GROUP * rows, wide), jnp.bfloat16),
        ],
        compiler_params=params,
        name="attention_forward",
    )(q, kv_all, kv_all, first)

    d_all = lax.dot_general(
        g_all, out_weight, (((1,), (1,)), ((), ())), preferred_element_type=jnp.float32
    ).astype(jnp.bfloat16)
    a_all = lax.all_to_all(a, "seq", split_axis=1, concat_axis=0, tiled=True)
    d = lax.all_to_all(d_all, "seq", split_axis=0, concat_axis=1, tiled=True)

    wo_grad = lax.dot_general(
        a_all, g_all, (((0,), (0,)), ((), ())), preferred_element_type=jnp.float32
    ).astype(jnp.bfloat16)
    weight_grad = lax.psum_scatter(wo_grad, "dp", scatter_dimension=1, tiled=True)
    product = jnp.dot(a_all, out_weight, preferred_element_type=jnp.float32)
    y = lax.psum_scatter(product.astype(jnp.bfloat16), "seq", scatter_dimension=0, tiled=True)

    k_out = pl.BlockSpec((wide, HEAD_SIZE), lambda i: (0, i))
    dq, dk, dv = pl.pallas_call(
        backward_kernel,
        grid=(KEY_VALUE_HEADS,),
        in_specs=[q_spec, k_spec, v_spec, q_spec, q_spec, p_spec],
        out_specs=[q_spec, k_out, k_out],
        out_shape=[
            jax.ShapeDtypeStruct(q.shape, jnp.bfloat16),
            jax.ShapeDtypeStruct((wide, kvw), jnp.bfloat16),
            jax.ShapeDtypeStruct((wide, kvw), jnp.bfloat16),
        ],
        compiler_params=params,
        name="attention_backward",
    )(q, kv_all, kv_all, a, d, p)
    dkv = jnp.concatenate([dk, dv], axis=1)
    total = dkv[halo * rows :].astype(jnp.float32)
    for j in range(1, halo + 1):
        part = lax.ppermute(
            dkv[(halo - j) * rows : (halo - j + 1) * rows],
            "seq",
            [(i + j, i) for i in range(n_seq - j)],
        )
        total = total + part.astype(jnp.float32)
    total = total.astype(jnp.bfloat16)
    return (
        y[None],
        dq[None],
        total[None, :, :kvw],
        total[None, :, kvw:],
        weight_grad.astype(jnp.float32),
    )


def solution(mesh):
    row = P("dp", "seq", None)
    return jax.shard_map(
        functools.partial(local, mesh.shape["seq"], mesh.shape["dp"]),
        mesh=mesh,
        in_specs=(row, row, row, P("seq", None), row, P("dp", None), P("dp", None)),
        out_specs=(row, row, row, row, P("seq", "dp")),
        check_vma=False,
    )
```

```python
import functools

import jax
import jax.numpy as jnp
from jax import lax
from jax.experimental import pallas as pl
from jax.experimental.pallas import tpu as pltpu
from jax.sharding import PartitionSpec as P

QUERY_HEADS = 32
KEY_VALUE_HEADS = 8
HEAD_SIZE = 128
GROUP = QUERY_HEADS // KEY_VALUE_HEADS
SCALE = HEAD_SIZE**-0.5


def row_starts(lengths, pack_order, win_rows):
    samples = lengths.shape[0]
    picked = jnp.sum(
        jnp.where(
            pack_order[:, None] == jnp.arange(samples, dtype=jnp.int32)[None, :],
            lengths[None, :],
            0,
        ),
        axis=1,
        dtype=jnp.int32,
    )
    at = jnp.arange(samples, dtype=jnp.int32)
    seg_ends = jnp.sum(jnp.where(at[None, :] <= at[:, None], picked[None, :], 0), axis=1)
    places = jnp.arange(win_rows, dtype=jnp.int32)
    return jnp.sum(
        jnp.where(seg_ends[None, :] <= places[:, None], picked[None, :], 0), axis=1, dtype=jnp.int32
    )


def nt(a, b):
    return lax.dot_general(a, b, (((1,), (1,)), ((), ())), preferred_element_type=jnp.float32)


def tn(a, b):
    return lax.dot_general(a, b, (((0,), (0,)), ((), ())), preferred_element_type=jnp.float32)


def stack_heads(x):
    return jnp.concatenate(
        [x[:, j * HEAD_SIZE : (j + 1) * HEAD_SIZE] for j in range(GROUP)], axis=0
    )


def unstack_heads(x, rows):
    return jnp.concatenate([x[j * rows : (j + 1) * rows] for j in range(GROUP)], axis=1)


def forward_kernel(q_ref, k_ref, v_ref, first_ref, a_ref, p_ref):
    rows, wide = q_ref.shape[0], k_ref.shape[0]
    back = wide - rows
    col = lax.broadcasted_iota(jnp.int32, (rows, wide), 1)
    row = lax.broadcasted_iota(jnp.int32, (rows, wide), 0) + back
    visible = (col >= first_ref[...]) & (col <= row)
    hidden = jnp.where(visible, 0.0, -jnp.inf)
    hidden = jnp.concatenate([hidden] * GROUP, axis=0)
    scores = nt(stack_heads(q_ref[...]), k_ref[...]) * SCALE + hidden
    e = jnp.exp(scores - jnp.max(scores, axis=-1, keepdims=True))
    p = (e / jnp.sum(e, axis=-1, keepdims=True)).astype(jnp.bfloat16)
    p_ref[0] = p
    a = jnp.dot(p, v_ref[...], preferred_element_type=jnp.float32).astype(jnp.bfloat16)
    a_ref[...] = unstack_heads(a, rows)


def backward_kernel(q_ref, k_ref, v_ref, a_ref, g_ref, p_ref, dq_ref, dk_ref, dv_ref):
    rows = q_ref.shape[0]
    q, g = stack_heads(q_ref[...]), stack_heads(g_ref[...])
    a = stack_heads(a_ref[...])
    p = p_ref[0]
    dot = jnp.sum(a.astype(jnp.float32) * g.astype(jnp.float32), axis=-1, keepdims=True)
    dp = nt(g, v_ref[...])
    ds = (p.astype(jnp.float32) * (dp - dot) * SCALE).astype(jnp.bfloat16)
    dq = jnp.dot(ds, k_ref[...], preferred_element_type=jnp.float32).astype(jnp.bfloat16)
    dq_ref[...] = unstack_heads(dq, rows)
    dk_ref[...] = tn(ds, q).astype(dk_ref.dtype)
    dv_ref[...] = tn(p, g).astype(dv_ref.dtype)


def weight_kernel(order_ref, a_ref, g_ref, o_ref):
    g = g_ref[0] if len(g_ref.shape) == 3 else g_ref[...]
    o_ref[0] = tn(a_ref[...], g).astype(o_ref.dtype)


def weight_blocks(a_all, g_all, order, part, parts, n_dp):
    win, cols = g_all.shape
    wide = cols // n_dp
    high = a_all.shape[1] // parts
    if wide % 128:
        g_all = jnp.transpose(g_all.reshape(win, n_dp, wide), (1, 0, 2))
        g_spec = pl.BlockSpec((1, win, wide), lambda i, o: (o[i], 0, 0))
    else:
        g_spec = pl.BlockSpec((win, wide), lambda i, o: (0, o[i]))
    count = order.shape[0]
    return pl.pallas_call(
        weight_kernel,
        grid_spec=pltpu.PrefetchScalarGridSpec(
            num_scalar_prefetch=1,
            grid=(count,),
            in_specs=[pl.BlockSpec((win, high), lambda i, o: (0, part)), g_spec],
            out_specs=pl.BlockSpec((1, high, wide), lambda i, o: (i, 0, 0)),
        ),
        out_shape=jax.ShapeDtypeStruct((count, high, wide), jnp.bfloat16),
        compiler_params=pltpu.CompilerParams(vmem_limit_bytes=32 << 20),
        cost_estimate=pl.CostEstimate(
            flops=2 * win * high * wide * count,
            bytes_accessed=2 * (win * high + win * wide * count + high * wide * count),
            transcendentals=0,
        ),
        name="weight_blocks",
    )(order, a_all, g_all)


def exchange(sent, kept, bit, n_dp):
    got = lax.ppermute(sent, "dp", [(i, i ^ bit) for i in range(n_dp)])
    return kept.astype(jnp.float32) + got.astype(jnp.float32)


def split_half(total):
    total = total.astype(jnp.bfloat16)
    half = total.shape[0] // 2
    return total[half:], total[:half]


def bit_orders(n_dp):
    bits = [1 << i for i in range(n_dp.bit_length() - 1)]
    return [bits, [bits[1], bits[0]] + bits[2:]]


def offsets(bits):
    found = [0]
    for bit in reversed(bits):
        found = found + [j ^ bit for j in found]
    return found


def local(n_seq, n_dp, queries, keys, values, out_weight, out_grad, lengths, pack_order):
    q, k, v, g = queries[0], keys[0], values[0], out_grad[0]
    rows = q.shape[0]
    win = rows * n_seq
    longest = win // 4
    halo = -(-(longest - 1) // rows)
    me = lax.axis_index("seq")
    starts = row_starts(lengths[0], pack_order[0], win)
    first = lax.dynamic_slice_in_dim(starts, me * rows, rows, 0) - (me - halo) * rows
    first = first[:, None]

    kv = jnp.concatenate([k, v], axis=1)
    pieces = [kv]
    for j in range(1, halo + 1):
        pieces.insert(0, lax.ppermute(kv, "seq", [(i, i + j) for i in range(n_seq - j)]))
    kv_all = jnp.concatenate(pieces, axis=0)
    wide = kv_all.shape[0]
    g_all = lax.all_gather(g, "seq", axis=0, tiled=True)

    kvw = KEY_VALUE_HEADS * HEAD_SIZE
    gw = GROUP * HEAD_SIZE
    q_spec = pl.BlockSpec((rows, gw), lambda i: (0, i))
    k_spec = pl.BlockSpec((wide, HEAD_SIZE), lambda i: (0, i))
    v_spec = pl.BlockSpec((wide, HEAD_SIZE), lambda i: (0, i + KEY_VALUE_HEADS))
    p_spec = pl.BlockSpec((1, GROUP * rows, wide), lambda i: (i, 0, 0))
    params = pltpu.CompilerParams(vmem_limit_bytes=32 << 20)
    a, p = pl.pallas_call(
        forward_kernel,
        grid=(KEY_VALUE_HEADS,),
        in_specs=[q_spec, k_spec, v_spec, pl.BlockSpec((rows, 1), lambda i: (0, 0))],
        out_specs=[q_spec, p_spec],
        out_shape=[
            jax.ShapeDtypeStruct(q.shape, jnp.bfloat16),
            jax.ShapeDtypeStruct((KEY_VALUE_HEADS, GROUP * rows, wide), jnp.bfloat16),
        ],
        compiler_params=params,
        name="attention_forward",
    )(q, kv_all, kv_all, first)

    a_all = lax.all_to_all(a, "seq", split_axis=1, concat_axis=0, tiled=True)
    d_all = lax.dot_general(
        g_all, out_weight, (((1,), (1,)), ((), ())), preferred_element_type=jnp.float32
    ).astype(jnp.bfloat16)
    a_all, d_all = lax.optimization_barrier((a_all, d_all))

    mine = lax.axis_index("dp")
    bit_lists = bit_orders(n_dp)
    orders = [mine ^ jnp.asarray(offsets(bits), jnp.int32) for bits in bit_lists]
    half = n_dp // 2
    parts = range(len(bit_lists))
    count = len(parts)
    sent = [weight_blocks(a_all, g_all, orders[i][half:], i, count, n_dp) for i in parts]
    kept = [weight_blocks(a_all, g_all, orders[i][:half], i, count, n_dp) for i in parts]
    product = jnp.dot(a_all, out_weight, preferred_element_type=jnp.float32)
    product = product.astype(jnp.bfloat16)
    y = lax.psum_scatter(product, "seq", scatter_dimension=0, tiled=True)

    d = None
    for level in range(len(bit_lists[0])):
        totals = [exchange(sent[i], kept[i], bit_lists[i][level], n_dp) for i in parts]
        if level == len(bit_lists[0]) - 1:
            break
        pairs = [split_half(total) for total in totals]
        sent, kept = [pair[0] for pair in pairs], [pair[1] for pair in pairs]
        if level == 0:
            q, sent = lax.optimization_barrier((q, sent))
            d = lax.all_to_all(d_all, "seq", split_axis=0, concat_axis=1, tiled=True)
    weight_grad = jnp.concatenate([total[0] for total in totals], axis=0)

    k_out = pl.BlockSpec((wide, HEAD_SIZE), lambda i: (0, i))
    dq, dk, dv = pl.pallas_call(
        backward_kernel,
        grid=(KEY_VALUE_HEADS,),
        in_specs=[q_spec, k_spec, v_spec, q_spec, q_spec, p_spec],
        out_specs=[q_spec, k_out, k_out],
        out_shape=[
            jax.ShapeDtypeStruct(q.shape, jnp.bfloat16),
            jax.ShapeDtypeStruct((wide, kvw), jnp.bfloat16),
            jax.ShapeDtypeStruct((wide, kvw), jnp.bfloat16),
        ],
        compiler_params=params,
        name="attention_backward",
    )(q, kv_all, kv_all, a, d, p)
    dkv = jnp.concatenate([dk, dv], axis=1)
    total = dkv[halo * rows :].astype(jnp.float32)
    for j in range(1, halo + 1):
        part = lax.ppermute(
            dkv[(halo - j) * rows : (halo - j + 1) * rows],
            "seq",
            [(i + j, i) for i in range(n_seq - j)],
        )
        total = total + part.astype(jnp.float32)
    total = total.astype(jnp.bfloat16)
    return (
        y[None],
        dq[None],
        total[None, :, :kvw],
        total[None, :, kvw:],
        weight_grad,
    )


def solution(mesh):
    row = P("dp", "seq", None)
    return jax.shard_map(
        functools.partial(local, mesh.shape["seq"], mesh.shape["dp"]),
        mesh=mesh,
        in_specs=(row, row, row, P("seq", None), row, P("dp", None), P("dp", None)),
        out_specs=(row, row, row, row, P("seq", "dp")),
        check_vma=False,
    )
```

```python
import functools

import jax
import jax.numpy as jnp
from jax import lax
from jax.experimental import pallas as pl
from jax.experimental.pallas import tpu as pltpu
from jax.sharding import PartitionSpec as P

QUERY_HEADS = 32
KEY_VALUE_HEADS = 8
HEAD_SIZE = 128
GROUP = QUERY_HEADS // KEY_VALUE_HEADS
SCALE = HEAD_SIZE**-0.5


def row_starts(lengths, pack_order, win_rows):
    samples = lengths.shape[0]
    picked = jnp.sum(
        jnp.where(
            pack_order[:, None] == jnp.arange(samples, dtype=jnp.int32)[None, :],
            lengths[None, :],
            0,
        ),
        axis=1,
        dtype=jnp.int32,
    )
    at = jnp.arange(samples, dtype=jnp.int32)
    seg_ends = jnp.sum(jnp.where(at[None, :] <= at[:, None], picked[None, :], 0), axis=1)
    places = jnp.arange(win_rows, dtype=jnp.int32)
    return jnp.sum(
        jnp.where(seg_ends[None, :] <= places[:, None], picked[None, :], 0), axis=1, dtype=jnp.int32
    )


def nt(a, b):
    return lax.dot_general(a, b, (((1,), (1,)), ((), ())), preferred_element_type=jnp.float32)


def tn(a, b):
    return lax.dot_general(a, b, (((0,), (0,)), ((), ())), preferred_element_type=jnp.float32)


def stack_heads(x):
    return jnp.concatenate(
        [x[:, j * HEAD_SIZE : (j + 1) * HEAD_SIZE] for j in range(GROUP)], axis=0
    )


def unstack_heads(x, rows):
    return jnp.concatenate([x[j * rows : (j + 1) * rows] for j in range(GROUP)], axis=1)


def forward_kernel(q_ref, k_ref, v_ref, first_ref, a_ref, p_ref):
    rows, wide = q_ref.shape[0], k_ref.shape[0]
    back = wide - rows
    col = lax.broadcasted_iota(jnp.int32, (rows, wide), 1)
    row = lax.broadcasted_iota(jnp.int32, (rows, wide), 0) + back
    visible = (col >= first_ref[...]) & (col <= row)
    hidden = jnp.where(visible, 0.0, -jnp.inf)
    hidden = jnp.concatenate([hidden] * GROUP, axis=0)
    scores = nt(stack_heads(q_ref[...]), k_ref[...]) * SCALE + hidden
    e = jnp.exp(scores - jnp.max(scores, axis=-1, keepdims=True))
    p = (e / jnp.sum(e, axis=-1, keepdims=True)).astype(jnp.bfloat16)
    p_ref[0] = p
    a = jnp.dot(p, v_ref[...], preferred_element_type=jnp.float32).astype(jnp.bfloat16)
    a_ref[...] = unstack_heads(a, rows)


def backward_kernel(q_ref, k_ref, v_ref, a_ref, g_ref, p_ref, dq_ref, dk_ref, dv_ref):
    rows = q_ref.shape[0]
    q, g = stack_heads(q_ref[...]), stack_heads(g_ref[...])
    a = stack_heads(a_ref[...])
    p = p_ref[0]
    dot = jnp.sum(a.astype(jnp.float32) * g.astype(jnp.float32), axis=-1, keepdims=True)
    dp = nt(g, v_ref[...])
    ds = (p.astype(jnp.float32) * (dp - dot) * SCALE).astype(jnp.bfloat16)
    dq = jnp.dot(ds, k_ref[...], preferred_element_type=jnp.float32).astype(jnp.bfloat16)
    dq_ref[...] = unstack_heads(dq, rows)
    dk_ref[...] = tn(ds, q).astype(dk_ref.dtype)
    dv_ref[...] = tn(p, g).astype(dv_ref.dtype)


def weight_kernel(order_ref, a_ref, g_ref, o_ref):
    g = g_ref[0] if len(g_ref.shape) == 3 else g_ref[...]
    o_ref[0] = tn(a_ref[...], g).astype(o_ref.dtype)


def weight_blocks(a_all, g_all, order, part, parts, n_dp):
    win, cols = g_all.shape
    wide = cols // n_dp
    high = a_all.shape[1] // parts
    if wide % 128:
        g_all = jnp.transpose(g_all.reshape(win, n_dp, wide), (1, 0, 2))
        g_spec = pl.BlockSpec((1, win, wide), lambda i, o: (o[i], 0, 0))
    else:
        g_spec = pl.BlockSpec((win, wide), lambda i, o: (0, o[i]))
    count = order.shape[0]
    return pl.pallas_call(
        weight_kernel,
        grid_spec=pltpu.PrefetchScalarGridSpec(
            num_scalar_prefetch=1,
            grid=(count,),
            in_specs=[pl.BlockSpec((win, high), lambda i, o: (0, part)), g_spec],
            out_specs=pl.BlockSpec((1, high, wide), lambda i, o: (i, 0, 0)),
        ),
        out_shape=jax.ShapeDtypeStruct((count, high, wide), jnp.bfloat16),
        compiler_params=pltpu.CompilerParams(vmem_limit_bytes=32 << 20),
        cost_estimate=pl.CostEstimate(
            flops=2 * win * high * wide * count,
            bytes_accessed=2 * (win * high + win * wide * count + high * wide * count),
            transcendentals=0,
        ),
        name="weight_blocks",
    )(order, a_all, g_all)


def exchange(sent, kept, bit, n_dp):
    got = lax.ppermute(sent, "dp", [(i, i ^ bit) for i in range(n_dp)])
    return kept.astype(jnp.float32) + got.astype(jnp.float32)


def split_half(total):
    total = total.astype(jnp.bfloat16)
    half = total.shape[0] // 2
    return total[half:], total[:half]


def bit_orders(n_dp):
    bits = [1 << i for i in range(n_dp.bit_length() - 1)]
    return [bits, [bits[1], bits[0]] + bits[2:]]


def offsets(bits):
    found = [0]
    for bit in reversed(bits):
        found = found + [j ^ bit for j in found]
    return found


def local(n_seq, n_dp, queries, keys, values, out_weight, out_grad, lengths, pack_order):
    q, k, v, g = queries[0], keys[0], values[0], out_grad[0]
    rows = q.shape[0]
    win = rows * n_seq
    longest = win // 4
    halo = -(-(longest - 1) // rows)
    me = lax.axis_index("seq")
    starts = row_starts(lengths[0], pack_order[0], win)
    first = lax.dynamic_slice_in_dim(starts, me * rows, rows, 0) - (me - halo) * rows
    first = first[:, None]

    kv = jnp.concatenate([k, v], axis=1)
    pieces = [kv]
    for j in range(1, halo + 1):
        pieces.insert(0, lax.ppermute(kv, "seq", [(i, i + j) for i in range(n_seq - j)]))
    kv_all = jnp.concatenate(pieces, axis=0)
    wide = kv_all.shape[0]
    g_all = lax.all_gather(g, "seq", axis=0, tiled=True)

    kvw = KEY_VALUE_HEADS * HEAD_SIZE
    gw = GROUP * HEAD_SIZE
    q_spec = pl.BlockSpec((rows, gw), lambda i: (0, i))
    k_spec = pl.BlockSpec((wide, HEAD_SIZE), lambda i: (0, i))
    v_spec = pl.BlockSpec((wide, HEAD_SIZE), lambda i: (0, i + KEY_VALUE_HEADS))
    p_spec = pl.BlockSpec((1, GROUP * rows, wide), lambda i: (i, 0, 0))
    params = pltpu.CompilerParams(vmem_limit_bytes=32 << 20)
    a, p = pl.pallas_call(
        forward_kernel,
        grid=(KEY_VALUE_HEADS,),
        in_specs=[q_spec, k_spec, v_spec, pl.BlockSpec((rows, 1), lambda i: (0, 0))],
        out_specs=[q_spec, p_spec],
        out_shape=[
            jax.ShapeDtypeStruct(q.shape, jnp.bfloat16),
            jax.ShapeDtypeStruct((KEY_VALUE_HEADS, GROUP * rows, wide), jnp.bfloat16),
        ],
        compiler_params=params,
        name="attention_forward",
    )(q, kv_all, kv_all, first)

    a_all = lax.all_to_all(a, "seq", split_axis=1, concat_axis=0, tiled=True)
    d_all = lax.dot_general(
        g_all, out_weight, (((1,), (1,)), ((), ())), preferred_element_type=jnp.float32
    ).astype(jnp.bfloat16)
    a_all, d_all = lax.optimization_barrier((a_all, d_all))

    mine = lax.axis_index("dp")
    bit_lists = bit_orders(n_dp)
    orders = [mine ^ jnp.asarray(offsets(bits), jnp.int32) for bits in bit_lists]
    half = n_dp // 2
    parts = range(len(bit_lists))
    count = len(parts)
    sent = [weight_blocks(a_all, g_all, orders[i][half:], i, count, n_dp) for i in parts]
    kept = [weight_blocks(a_all, g_all, orders[i][:half], i, count, n_dp) for i in parts]
    a_all, sent[0] = lax.optimization_barrier((a_all, sent[0]))
    product = jnp.dot(a_all, out_weight, preferred_element_type=jnp.float32)
    product = product.astype(jnp.bfloat16)
    y = lax.psum_scatter(product, "seq", scatter_dimension=0, tiled=True)

    d = None
    for level in range(len(bit_lists[0])):
        totals = [exchange(sent[i], kept[i], bit_lists[i][level], n_dp) for i in parts]
        if level == len(bit_lists[0]) - 1:
            break
        pairs = [split_half(total) for total in totals]
        sent, kept = [pair[0] for pair in pairs], [pair[1] for pair in pairs]
        if level == 0:
            q, sent = lax.optimization_barrier((q, sent))
            d = lax.all_to_all(d_all, "seq", split_axis=0, concat_axis=1, tiled=True)
    weight_grad = jnp.concatenate([total[0] for total in totals], axis=0)

    k_out = pl.BlockSpec((wide, HEAD_SIZE), lambda i: (0, i))
    dq, dk, dv = pl.pallas_call(
        backward_kernel,
        grid=(KEY_VALUE_HEADS,),
        in_specs=[q_spec, k_spec, v_spec, q_spec, q_spec, p_spec],
        out_specs=[q_spec, k_out, k_out],
        out_shape=[
            jax.ShapeDtypeStruct(q.shape, jnp.bfloat16),
            jax.ShapeDtypeStruct((wide, kvw), jnp.bfloat16),
            jax.ShapeDtypeStruct((wide, kvw), jnp.bfloat16),
        ],
        compiler_params=params,
        name="attention_backward",
    )(q, kv_all, kv_all, a, d, p)
    dkv = jnp.concatenate([dk, dv], axis=1)
    total = dkv[halo * rows :].astype(jnp.float32)
    for j in range(1, halo + 1):
        part = lax.ppermute(
            dkv[(halo - j) * rows : (halo - j + 1) * rows],
            "seq",
            [(i + j, i) for i in range(n_seq - j)],
        )
        total = total + part.astype(jnp.float32)
    total = total.astype(jnp.bfloat16)
    return (
        y[None],
        dq[None],
        total[None, :, :kvw],
        total[None, :, kvw:],
        weight_grad,
    )


def solution(mesh):
    row = P("dp", "seq", None)
    return jax.shard_map(
        functools.partial(local, mesh.shape["seq"], mesh.shape["dp"]),
        mesh=mesh,
        in_specs=(row, row, row, P("seq", None), row, P("dp", None), P("dp", None)),
        out_specs=(row, row, row, row, P("seq", "dp")),
        check_vma=False,
    )
```
